32 devices in a mesh: groups: 2 (over y), expert: 4 (over z), tensor: 2 (over x), seq: 2 (over core).
Axes of the slice: x: 2, y: 2, z: 4, core: 2. Of those that a mesh axis runs over, the one named last changes fastest.
Arguments:
- tokens: bfloat16 [4096, 4096], P(('groups', 'expert', 'seq'), 'tensor'), parts along dimension 0, may hold values from -6 to 6
- gate_values: float32 [4096, 2], P(('groups', 'expert', 'seq')), parts along dimension 0, may hold values from 0.2 to 1.2
- routes: int32 [4096, 2], P(('groups', 'expert', 'seq')), parts along dimension 0, may hold values from 0 to 3, all different within a row; in each aligned block of 256 rows (0 to 255, 256 to 511, ...) at most 192 rows name the same one
- w_down: bfloat16 [4096, 1024], P('tensor'), may hold values from -0.09375 to 0.09375
- expert_gate: bfloat16 [4, 1024, 2048], P('expert', None, 'tensor'), may hold values from -0.1875 to 0.1875
- expert_up: bfloat16 [4, 1024, 2048], P('expert', None, 'tensor'), may hold values from -0.1875 to 0.1875
- expert_down: bfloat16 [4, 2048, 1024], P('expert', 'tensor'), may hold values from -0.125 to 0.125
- w_up: bfloat16 [1024, 4096], P(None, 'tensor'), may hold values from -0.1875 to 0.1875
Outputs:
- layer_out: bfloat16 [4096, 4096], P(('groups', 'expert', 'seq'), 'tensor'), parts along dimension 0
The draws below stay inside these ranges and needn't reach their ends.
There are 2 independent parts, one for each index of `groups`. The reference program is written for one: setup_inputs(seed, part) draws one part's arguments, and reference() takes and returns one part's arrays. A program takes and returns all parts, laid end to end along the dimension named above; an argument that names none is the same for every part. Nothing has to cross between parts.
Inputs may be any that keep to these rules, and one draw needn't show every extreme that they name: `routes`: in the 256 rows of one device no expert is named by more than 192 pairs, and one expert is named by exactly 192; a row names 2 different experts.
All inputs are finite; a program needn't handle non-finite values.
Results may differ from the reference program's by a relative error of at most 0.014.
Values may be sent and summed in bfloat16 or wider, within the bound.
A program may use at most 64 MiB of HBM per device.

```python
import math
import jax
import jax.numpy as jnp
import numpy as np
from jax import lax

D = 4096
LAT = 1024
FF = 2048
TOPK = 2
TOK_DEV = 256
EXPERTS = 4
TOKENS = 2048
CAP = 192


def steps_of(stream_key, extent, cuts, low, high):
    def one(dim, blocks):
        draws = jax.random.uniform(jax.random.fold_in(jax.random.fold_in(stream_key, 6), dim), (blocks,), jnp.float32, low / len(cuts), high / len(cuts))
        return jnp.repeat(jnp.exp(draws), extent[dim] // blocks).reshape((-1,) + (1,) * (len(extent) - dim - 1))

    level = one(*cuts[0])
    for cut in cuts[1:]:
        level = level * one(*cut)
    return level


def routed_block(stream_key, own, number, rows, number_of, top, most, skew):
    sequence = jax.random.permutation(stream_key, number_of)
    heavy_load, ordinary = shares(number_of, rows * top, most, skew, True), shares(number_of, rows * top, most, skew, False)
    places = jnp.arange(number_of)

    def named(tallies, rotation):
        used = int((tallies > 0).sum())
        fixed = max(1, used // 4)
        passed = fixed + (places - fixed + rotation * (used - fixed)) % max(1, number_of - fixed)
        return jnp.zeros((number_of,), jnp.int32).at[sequence[jnp.where(places < fixed, places, passed)]].set(jnp.asarray(tallies, jnp.int32))

    tallies = jnp.where(number % 4 == 0, named(heavy_load, number // 4), named(ordinary, number - number // 4 - 1))
    mixed = jax.random.permutation(jax.random.fold_in(own, 3), number_of)
    source_of, sink = mixed[0:number_of // 2 * 2:2], mixed[1:number_of // 2 * 2:2]
    slack = jnp.minimum(tallies[source_of] - 1, most - tallies[sink]) // 2
    slack = jnp.where((source_of == sequence[0]) | (sink == sequence[0]) | (tallies[sink] == 0), 0, jnp.maximum(slack, 0))
    passed = jax.random.randint(jax.random.fold_in(own, 4), (number_of // 2,), 0, 1 << 20) % (slack + 1)
    tallies = tallies.at[source_of].add(-passed).at[sink].add(passed)
    labels = jnp.searchsorted(jnp.cumsum(tallies), jnp.arange(rows * top), side="right").astype(jnp.int32)
    grid = labels.reshape(top, rows).T
    grid = grid[jax.random.permutation(jax.random.fold_in(own, 1), rows)]
    rotation = jax.random.randint(jax.random.fold_in(own, 2), (rows, 1), 0, top)
    return jnp.take_along_axis(grid, (jnp.arange(top)[None, :] + rotation) % top, axis=1)


def shares(amount, total, limit, slope, full):
    portions = [(1 << 20) // math.isqrt(grade ** slope) + 1 for grade in range(1, amount + 1)]
    largest = limit if full else min(limit, max(-(-total // amount), total * portions[0] // sum(portions)))
    least = 1 if total - largest >= amount - 1 else 0
    holding, spare = [largest] + [least] * (amount - 1), total - largest - least * (amount - 1)
    while spare > 0:
        movable = [i for i in range(1, amount) if holding[i] < largest] or [i for i in range(1, amount) if holding[i] < limit]
        mass, left = sum([portions[i] for i in movable]), spare
        for i in movable:
            more = min(limit - holding[i], max(1, left * portions[i] // mass), spare)
            holding[i] = holding[i] + more
            spare = spare - more
    return np.array(holding)


def gaussian(key, dims, width, bound, split=(), kind=jnp.bfloat16):
    values = jax.random.normal(key, dims, jnp.float32) * width
    if len(split) > 0:
        values = steps_of(key, dims, split, -0.22, 0.18) * values
    return jnp.clip(values, min=-bound, max=bound).astype(kind)


def setup_inputs(seed: int = 0, part: int = 0) -> dict:
    key_list = jax.random.split(jax.random.key(seed), 9)
    own_keys = jax.random.split(jax.random.fold_in(key_list[8], part), 9)
    tokens = gaussian(own_keys[0], (TOKENS, D), 1.0, 6.0, ((0, 8), (1, 2)))
    gate_values = jnp.clip(0.2 + 1 * jax.random.uniform(own_keys[1], (TOKENS, TOPK), jnp.float32) ** steps_of(own_keys[1], (TOKENS, TOPK), ((0, 8),), -0.2, 0.2), 0.2, 1.2)
    routes_keys = jax.random.split(jax.random.fold_in(own_keys[2], 1), TOKENS // TOK_DEV)
    routes_turns = jax.random.permutation(jax.random.fold_in(own_keys[2], 3), TOKENS // TOK_DEV)
    routes = jax.vmap(lambda own, number: routed_block(jax.random.fold_in(own_keys[2], 2), own, number, TOK_DEV, EXPERTS, TOPK, CAP, 2))(routes_keys, routes_turns).reshape((TOKENS, TOPK))
    w_down = gaussian(key_list[3], (D, LAT), D ** -0.5, 0.09375, ((0, 2),))
    expert_gate = gaussian(key_list[4], (EXPERTS, LAT, FF), LAT ** -0.5, 0.1875, ((0, 4), (2, 2)))
    expert_up = gaussian(key_list[5], (EXPERTS, LAT, FF), LAT ** -0.5, 0.1875, ((0, 4), (2, 2)))
    expert_down = gaussian(key_list[6], (EXPERTS, FF, LAT), FF ** -0.5, 0.125, ((0, 4), (1, 2)))
    w_up = gaussian(key_list[7], (LAT, D), LAT ** -0.5, 0.1875, ((1, 2),))
    return dict(tokens=tokens, gate_values=gate_values, routes=routes, w_down=w_down, expert_gate=expert_gate, expert_up=expert_up, expert_down=expert_down, w_up=w_up)


def slot_ids(block_routes):
    chosen = block_routes.reshape(-1)
    onehot = (chosen[:, None] == jnp.arange(EXPERTS, dtype=jnp.int32)[None, :]).astype(jnp.int32)
    earlier = jnp.cumsum(onehot, axis=0) - onehot
    slot_pos = jnp.sum(earlier * onehot, axis=1)
    return (chosen * CAP + slot_pos).astype(jnp.int32)


def run_expert(inputs):
    inbox, gate_w, up_w, down_w = inputs
    gate_act = jnp.dot(inbox, gate_w, preferred_element_type=jnp.float32)
    up_act = jnp.dot(inbox, up_w, preferred_element_type=jnp.float32)
    hidden = (jax.nn.silu(gate_act) * up_act).astype(jnp.bfloat16)
    return jnp.dot(hidden, down_w, preferred_element_type=jnp.float32)


def reference(tokens, gate_values, routes, w_down, expert_gate, expert_up, expert_down, w_up):
    blocks = TOKENS // TOK_DEV
    pairs = TOK_DEV * TOPK
    latent = jnp.dot(tokens, w_down, preferred_element_type=jnp.float32).astype(jnp.bfloat16)
    latent_blocks = latent.reshape(blocks, TOK_DEV, LAT)
    flat_ids = jax.vmap(slot_ids)(routes.reshape(blocks, TOK_DEV, TOPK))
    token_of = jnp.arange(pairs, dtype=jnp.int32) // TOPK

    def fill(block_latent, block_ids):
        empty = jnp.zeros((EXPERTS * CAP, LAT), jnp.bfloat16)
        return empty.at[block_ids].set(block_latent[token_of])

    inbox = jax.vmap(fill)(latent_blocks, flat_ids)
    inbox = inbox.reshape(blocks, EXPERTS, CAP, LAT).transpose(1, 0, 2, 3).reshape(EXPERTS, blocks * CAP, LAT)
    expert_out = lax.map(run_expert, (inbox, expert_gate, expert_up, expert_down))
    expert_out = expert_out.reshape(EXPERTS, blocks, CAP, LAT).transpose(1, 0, 2, 3).reshape(blocks, EXPERTS * CAP, LAT)
    picked = jax.vmap(lambda outs, ids: outs[ids])(expert_out, flat_ids)
    weights = gate_values.reshape(blocks, pairs).astype(jnp.float32)
    combined = (picked * weights[:, :, None]).reshape(blocks, TOK_DEV, TOPK, LAT).sum(axis=2)
    combined = combined.reshape(TOKENS, LAT).astype(jnp.bfloat16)
    return jnp.dot(combined, w_up, preferred_element_type=jnp.float32).astype(jnp.bfloat16)
```

```python
import functools

import jax
import jax.numpy as jnp
from jax import lax
from jax.experimental import pallas as pl
from jax.experimental.pallas import tpu as pltpu
from jax.sharding import PartitionSpec as P

MESH = pl.DeviceIdType.MESH
F32 = jnp.float32
BF16 = jnp.bfloat16


def flip(index, step, count):
    out, bit = 0, 1
    while bit < count:
        out = out + ((index // bit + (step // bit) % 2) % 2) * bit
        bit *= 2
    return out


def kernel(
    n_exp, n_ten, cap,
    tokens, gates, routes, w_down, w_gate, w_upx, w_dn, w_up, out,
    tok_v, wd_v, wg_v, wu_v, wdn_v, wup_v,
    lat_send, lat_recv, outbox, inbox, o_own, o_send, o_recv, r_send, r_recv, comb, acc, out_v,
    load_sem, rs_s, rs_r, z_s, z_r, ag_s, ag_r, os_s, os_r, rt_s, rt_r, fa_s, fa_r, st_sem,
):
    me = lax.axis_index("expert")
    ten = lax.axis_index("tensor")
    rows = tok_v.shape[0]
    lat = wd_v.shape[1]
    lw = lat // n_ten

    def cols(t):
        return pl.ds(pl.multiple_of(t * lw, 128), lw)

    mine = cols(ten)

    loads = []
    for i, (src, dst) in enumerate(
        ((tokens, tok_v), (w_down, wd_v), (w_gate.at[0], wg_v), (w_upx.at[0], wu_v), (w_dn.at[0], wdn_v), (w_up, wup_v))
    ):
        c = pltpu.make_async_copy(src, dst, load_sem.at[i])
        c.start()
        loads.append(c)

    barrier = pltpu.get_barrier_semaphore()
    for k in range(1, n_exp):
        pl.semaphore_signal(barrier, inc=1, device_id={"expert": flip(me, k, n_exp)}, device_id_type=MESH)
    for j in range(1, n_ten):
        pl.semaphore_signal(barrier, inc=1, device_id={"tensor": (ten + j) % n_ten}, device_id_type=MESH)

    lanes = 128
    ids = lax.broadcasted_iota(jnp.int32, (rows, lanes), 1)
    first, second = routes[:, 0:1], routes[:, 1:2]
    named = jnp.where((first == ids) | (second == ids), 1.0, 0.0).astype(F32)
    r0 = lax.broadcasted_iota(jnp.int32, (rows, rows), 0)
    r1 = lax.broadcasted_iota(jnp.int32, (rows, rows), 1)
    below = jnp.where(r1 < r0, 1.0, 0.0).astype(BF16)
    slot = jnp.dot(below, named.astype(BF16), preferred_element_type=F32)
    code = jnp.where(named > 0.5, slot, -1.0)
    code_t = code.T
    sub = lax.broadcasted_iota(jnp.int32, (lanes, rows), 0)

    def select_rows(e):
        line = jnp.sum(jnp.where(sub == e, code_t, 0.0), axis=0, keepdims=True)
        at = lax.broadcasted_iota(jnp.int32, (cap, rows), 0).astype(F32)
        return jnp.where(at == line, 1.0, 0.0).astype(BF16)

    def place_rows(e):
        line = jnp.sum(jnp.where(ids == e, code, 0.0), axis=1, keepdims=True)
        at = lax.broadcasted_iota(jnp.int32, (rows, cap), 1).astype(F32)
        return jnp.where(at == line, 1.0, 0.0).astype(BF16)

    def weight(e):
        return jnp.where(first == e, gates[:, 0:1], 0.0) + jnp.where(second == e, gates[:, 1:2], 0.0)

    pl.semaphore_wait(barrier, n_exp - 1 + n_ten - 1)

    loads[0].wait()
    loads[1].wait()

    def remote(src, dst, s, r, to):
        return pltpu.make_async_remote_copy(
            src_ref=src, dst_ref=dst, send_sem=s, recv_sem=r, device_id=to, device_id_type=MESH
        )

    rs = {}
    for j in range(1, n_ten):
        to = (ten + j) % n_ten
        lat_send[j] = jnp.dot(tok_v[...], wd_v[:, cols(to)], preferred_element_type=F32).astype(BF16)
        rs[j] = remote(lat_send.at[j], lat_recv.at[j], rs_s.at[j], rs_r.at[j], {"tensor": to})
        rs[j].start()
    total = jnp.dot(tok_v[...], wd_v[:, mine], preferred_element_type=F32)
    for j in range(1, n_ten):
        rs[j].wait()
        total = total + lat_recv[j].astype(F32)
    latent = total.astype(BF16)

    order = list(range(n_exp // 2, n_exp)) + list(range(n_exp // 2 - 1, 0, -1))
    z, ag, osd, rt = {}, {}, {}, {}

    def gather(k):
        for j in range(1, n_ten):
            to = (ten + j) % n_ten
            here = inbox.at[k, :, mine]
            ag[k, j] = remote(here, here, ag_s.at[k, j], ag_r.at[k, j], {"tensor": to})
            ag[k, j].start()

    for k in order:
        e = flip(me, k, n_exp)
        outbox[k] = jnp.dot(select_rows(e), latent, preferred_element_type=F32).astype(BF16)
        z[k] = remote(outbox.at[k], inbox.at[k, :, mine], z_s.at[k], z_r.at[k], {"expert": e})
        z[k].start()
    inbox[0, :, mine] = jnp.dot(select_rows(me), latent, preferred_element_type=F32).astype(BF16)
    gather(0)

    for i in range(2, 5):
        loads[i].wait()

    def stage_a(k):
        z[k].wait()
        gather(k)

    def stage_b(k):
        for j in range(1, n_ten):
            ag[k, j].wait()
        x = inbox[k]
        g = jnp.dot(x, wg_v[...], preferred_element_type=F32)
        u = jnp.dot(x, wu_v[...], preferred_element_type=F32)
        h = (g / (1.0 + jnp.exp(-g)) * u).astype(BF16)
        for j in range(1, n_ten):
            to = (ten + j) % n_ten
            o_send[k, j] = jnp.dot(h, wdn_v[:, cols(to)], preferred_element_type=F32).astype(BF16)
            osd[k, j] = remote(o_send.at[k, j], o_recv.at[k, j], os_s.at[k, j], os_r.at[k, j], {"tensor": to})
            osd[k, j].start()
        o_own[k] = jnp.dot(h, wdn_v[:, mine], preferred_element_type=F32)

    def stage_c(k):
        y = o_own[k]
        for j in range(1, n_ten):
            osd[k, j].wait()
            y = y + o_recv[k, j].astype(F32)
        if k == 0:
            r_recv[0] = y.astype(BF16)
            return
        r_send[k] = y.astype(BF16)
        rt[k] = remote(r_send.at[k], r_recv.at[k], rt_s.at[k], rt_r.at[k], {"expert": flip(me, k, n_exp)})
        rt[k].start()

    line = [0] + order
    stage_b(0)
    for i in range(1, n_exp):
        stage_a(line[i])
        stage_c(line[i - 1])
        stage_b(line[i])
    stage_c(line[-1])

    both = jnp.zeros((rows, lw), F32)
    for k in line:
        e = flip(me, k, n_exp)
        if k:
            rt[k].wait()
        both = both + weight(e) * jnp.dot(place_rows(e), r_recv[k], preferred_element_type=F32)
    comb[:, mine] = both.astype(BF16)
    fa = {}
    for j in range(1, n_ten):
        to = (ten + j) % n_ten
        fa[j] = remote(comb.at[:, mine], comb.at[:, mine], fa_s.at[j], fa_r.at[j], {"tensor": to})
        fa[j].start()
    loads[5].wait()

    def up_rows(t):
        return pl.ds(pl.multiple_of(t * lw, 128), lw)

    acc[...] = jnp.dot(comb[:, mine], wup_v[up_rows(ten), :], preferred_element_type=F32)
    for j in range(1, n_ten):
        fa[j].wait()
    width = out_v.shape[1]
    parts = 2 if width >= 512 else 1
    pw = width // parts
    stores = []
    for p in range(parts):
        span = slice(p * pw, (p + 1) * pw)
        y = acc[:, span]
        for j in range(1, n_ten):
            t = (ten + n_ten - j) % n_ten
            y = y + jnp.dot(comb[:, cols(t)], wup_v[up_rows(t), span], preferred_element_type=F32)
        out_v[:, span] = y.astype(BF16)
        c = pltpu.make_async_copy(out_v.at[:, span], out.at[:, span], st_sem.at[p])
        c.start()
        stores.append(c)
    for c in stores:
        c.wait()


def local(tokens, gate_values, routes, w_down, expert_gate, expert_up, expert_down, w_up):
    rows, top = routes.shape
    lat = w_down.shape[1]
    n_exp = lax.axis_size("expert")
    n_ten = lax.axis_size("tensor")
    exp_dev = expert_gate.shape[0]
    total = n_exp * exp_dev
    cap = n_ten * ((3 * rows * top + 2 * total * n_ten - 1) // (2 * total * n_ten))
    lw = lat // n_ten
    width = w_up.shape[1]
    dma = pltpu.SemaphoreType.DMA
    any_spec = pl.BlockSpec(memory_space=pl.ANY)
    vmem = pl.BlockSpec(memory_space=pltpu.VMEM)
    return pl.pallas_call(
        functools.partial(kernel, n_exp, n_ten, cap),
        out_shape=jax.ShapeDtypeStruct((rows, width), BF16),
        in_specs=[any_spec, vmem, vmem] + [any_spec] * 5,
        out_specs=any_spec,
        scratch_shapes=[
            pltpu.VMEM(tokens.shape, BF16),
            pltpu.VMEM(w_down.shape, BF16),
            pltpu.VMEM(expert_gate.shape[1:], BF16),
            pltpu.VMEM(expert_up.shape[1:], BF16),
            pltpu.VMEM(expert_down.shape[1:], BF16),
            pltpu.VMEM(w_up.shape, BF16),
            pltpu.VMEM((n_ten, rows, lw), BF16),
            pltpu.VMEM((n_ten, rows, lw), BF16),
            pltpu.VMEM((n_exp, cap, lw), BF16),
            pltpu.VMEM((n_exp, cap, lat), BF16),
            pltpu.VMEM((n_exp, cap, lw), F32),
            pltpu.VMEM((n_exp, n_ten, cap, lw), BF16),
            pltpu.VMEM((n_exp, n_ten, cap, lw), BF16),
            pltpu.VMEM((n_exp, cap, lw), BF16),
            pltpu.VMEM((n_exp, cap, lw), BF16),
            pltpu.VMEM((rows, lat), BF16),
            pltpu.VMEM((rows, width), F32),
            pltpu.VMEM((rows, width), BF16),
            dma((6,)),
            dma((n_ten,)), dma((n_ten,)),
            dma((n_exp,)), dma((n_exp,)),
            dma((n_exp, n_ten)), dma((n_exp, n_ten)),
            dma((n_exp, n_ten)), dma((n_exp, n_ten)),
            dma((n_exp,)), dma((n_exp,)),
            dma((n_ten,)), dma((n_ten,)),
            dma((2,)),
        ],
        compiler_params=pltpu.CompilerParams(
            collective_id=0, has_side_effects=True, vmem_limit_bytes=56 * 1024 * 1024
        ),
        name="moe_layer",
    )(tokens, gate_values, routes, w_down, expert_gate, expert_up, expert_down, w_up)


def solution(mesh):
    return jax.shard_map(
        local,
        mesh=mesh,
        in_specs=(
            P(("groups", "expert", "seq"), "tensor"),
            P(("groups", "expert", "seq"), None),
            P(("groups", "expert", "seq"), None),
            P("tensor", None),
            P("expert", None, "tensor"),
            P("expert", None, "tensor"),
            P("expert", "tensor", None),
            P(None, "tensor"),
        ),
        out_specs=P(("groups", "expert", "seq"), "tensor"),
        check_vma=False,
    )
```

```python
import functools

import jax
import jax.numpy as jnp
from jax import lax
from jax.experimental import pallas as pl
from jax.experimental.pallas import tpu as pltpu
from jax.sharding import PartitionSpec as P

MESH = pl.DeviceIdType.MESH
F32 = jnp.float32
BF16 = jnp.bfloat16


def flip(index, step, count):
    out, bit = 0, 1
    while bit < count:
        out = out + ((index // bit + (step // bit) % 2) % 2) * bit
        bit *= 2
    return out


def kernel(
    n_exp, n_ten, cap,
    tokens, gates, routes, w_down, w_gate, w_upx, w_dn, w_up, out,
    tok_v, wd_v, wg_v, wu_v, wdn_v, wup_v,
    lat_send, lat_recv, outbox, inbox, o_own, o_send, o_recv, r_send, r_recv, comb, acc, out_v,
    load_sem, rs_s, rs_r, z_s, z_r, ag_s, ag_r, os_s, os_r, rt_s, rt_r, fa_s, fa_r, st_sem,
):
    me = lax.axis_index("expert")
    ten = lax.axis_index("tensor")
    rows = tok_v.shape[0]
    lat = wd_v.shape[1]
    lw = lat // n_ten

    def cols(t):
        return pl.ds(pl.multiple_of(t * lw, 128), lw)

    mine = cols(ten)

    def load(i, src, dst):
        c = pltpu.make_async_copy(src, dst, load_sem.at[i])
        c.start()
        return c

    peers = [(ten + j) % n_ten for j in range(1, n_ten)] + [ten]
    load_tok = load(5, tokens, tok_v)
    load_down = [load(6 + i, w_down.at[:, cols(t)], wd_v.at[:, cols(t)]) for i, t in enumerate(peers)]

    barrier = pltpu.get_barrier_semaphore()
    for k in range(1, n_exp):
        pl.semaphore_signal(barrier, inc=1, device_id={"expert": flip(me, k, n_exp)}, device_id_type=MESH)
    for j in range(1, n_ten):
        pl.semaphore_signal(barrier, inc=1, device_id={"tensor": (ten + j) % n_ten}, device_id_type=MESH)

    lanes = 128
    ids = lax.broadcasted_iota(jnp.int32, (rows, lanes), 1)
    sub = lax.broadcasted_iota(jnp.int32, (lanes, rows), 0)
    first, second = routes[0:1, :], routes[1:2, :]
    named = jnp.where((first == sub) | (second == sub), 1.0, 0.0).astype(F32)
    r0 = lax.broadcasted_iota(jnp.int32, (rows, rows), 0)
    r1 = lax.broadcasted_iota(jnp.int32, (rows, rows), 1)
    above = jnp.where(r0 < r1, 1.0, 0.0).astype(BF16)
    slot = jnp.dot(named.astype(BF16), above, preferred_element_type=F32)
    code_t = jnp.where(named > 0.5, slot, -1.0)
    code = code_t.T
    share = (jnp.where(first == sub, gates[0:1, :], 0.0) + jnp.where(second == sub, gates[1:2, :], 0.0)).T

    def select_rows(e):
        line = jnp.sum(jnp.where(sub == e, code_t, 0.0), axis=0, keepdims=True)
        at = lax.broadcasted_iota(jnp.int32, (cap, rows), 0).astype(F32)
        return jnp.where(at == line, 1.0, 0.0).astype(BF16)

    def place_rows(e):
        line = jnp.sum(jnp.where(ids == e, code, 0.0), axis=1, keepdims=True)
        at = lax.broadcasted_iota(jnp.int32, (rows, cap), 1).astype(F32)
        return jnp.where(at == line, 1.0, 0.0).astype(BF16)

    def weight(e):
        return jnp.sum(jnp.where(ids == e, share, 0.0), axis=1, keepdims=True)

    sends = []

    def remote(src, dst, s, r, to):
        c = pltpu.make_async_remote_copy(
            src_ref=src, dst_ref=dst, send_sem=s, recv_sem=r, device_id=to, device_id_type=MESH
        )
        c.start()
        sends.append(c)
        return c

    load_tok.wait()
    for j in range(1, n_ten):
        load_down[j - 1].wait()
        lat_send[j] = jnp.dot(tok_v[...], wd_v[:, cols(peers[j - 1])], preferred_element_type=F32).astype(BF16)
    pl.semaphore_wait(barrier, n_exp - 1 + n_ten - 1)
    rs = {}
    for j in range(1, n_ten):
        rs[j] = remote(lat_send.at[j], lat_recv.at[j], rs_s.at[j], rs_r.at[j], {"tensor": peers[j - 1]})
    load_down[-1].wait()
    weights = ((w_gate.at[0], wg_v), (w_upx.at[0], wu_v), (w_dn.at[0], wdn_v), (w_up, wup_v))
    loads = [load(i, src, dst) for i, (src, dst) in enumerate(weights)]
    total = jnp.dot(tok_v[...], wd_v[:, mine], preferred_element_type=F32)
    for j in range(1, n_ten):
        rs[j].wait_recv()
        total = total + lat_recv[j].astype(F32)
    latent = total.astype(BF16)

    order = list(range(1,n_exp))
    z, ag, osd, rt = {}, {}, {}, {}

    def gather(k):
        for j in range(1, n_ten):
            to = (ten + j) % n_ten
            here = inbox.at[k, :, mine]
            ag[k, j] = remote(here, here, ag_s.at[k, j], ag_r.at[k, j], {"tensor": to})

    late = n_exp - 1

    def dispatch(k):
        to = {"expert": flip(me, k, n_exp)}
        z[k] = remote(outbox.at[k], inbox.at[k, :, mine], z_s.at[k], z_r.at[k], to)

    for k in order:
        e = flip(me, k, n_exp)
        outbox[k] = jnp.dot(select_rows(e), latent, preferred_element_type=F32).astype(BF16)
        if k != late:
            dispatch(k)
    inbox[0, :, mine] = jnp.dot(select_rows(me), latent, preferred_element_type=F32).astype(BF16)
    gather(0)

    for i in range(3):
        loads[i].wait()

    def stage_a(k):
        z[k].wait_recv()
        gather(k)

    def stage_b(k):
        for j in range(1, n_ten):
            ag[k, j].wait_recv()
        x = inbox[k]
        g = jnp.dot(x, wg_v[...], preferred_element_type=F32)
        u = jnp.dot(x, wu_v[...], preferred_element_type=F32)
        h = (g / (1.0 + jnp.exp(-g)) * u).astype(BF16)
        for j in range(1, n_ten):
            to = (ten + j) % n_ten
            o_send[k, j] = jnp.dot(h, wdn_v[:, cols(to)], preferred_element_type=F32).astype(BF16)
            osd[k, j] = remote(o_send.at[k, j], o_recv.at[k, j], os_s.at[k, j], os_r.at[k, j], {"tensor": to})
        o_own[k] = jnp.dot(h, wdn_v[:, mine], preferred_element_type=F32)

    def stage_c(k):
        y = o_own[k]
        for j in range(1, n_ten):
            osd[k, j].wait_recv()
            y = y + o_recv[k, j].astype(F32)
        if k == 0:
            r_recv[0] = y.astype(BF16)
            return
        r_send[k] = y.astype(BF16)
        rt[k] = remote(r_send.at[k], r_recv.at[k], rt_s.at[k], rt_r.at[k], {"expert": flip(me, k, n_exp)})

    both = jnp.zeros((rows, lw), F32)

    def stage_d(k, both):
        e = flip(me, k, n_exp)
        if k:
            rt[k].wait_recv()
        return both + weight(e) * jnp.dot(place_rows(e), r_recv[k], preferred_element_type=F32)

    line = [0] + order
    dispatch(late)
    stage_b(0)
    stage_a(line[1])
    for i in range(1, n_exp):
        if i + 1 < late:
            stage_a(line[i + 1])
        if i == late:
            stage_a(late)
        stage_c(line[i - 1])
        stage_b(line[i])
    both = stage_d(line[0], both)
    stage_c(line[-1])
    for k in line[1:]:
        both = stage_d(k, both)
    comb[:, mine] = both.astype(BF16)
    fa = {}
    for j in range(1, n_ten):
        to = (ten + j) % n_ten
        fa[j] = remote(comb.at[:, mine], comb.at[:, mine], fa_s.at[j], fa_r.at[j], {"tensor": to})
    loads[3].wait()

    def up_rows(t):
        return pl.ds(pl.multiple_of(t * lw, 128), lw)

    acc[...] = jnp.dot(comb[:, mine], wup_v[up_rows(ten), :], preferred_element_type=F32)
    for j in range(1, n_ten):
        fa[j].wait_recv()
    width = out_v.shape[1]
    parts = 2 if width >= 512 else 1
    pw = width // parts
    stores = []
    for p in range(parts):
        span = slice(p * pw, (p + 1) * pw)
        y = acc[:, span]
        for j in range(1, n_ten):
            t = (ten + n_ten - j) % n_ten
            y = y + jnp.dot(comb[:, cols(t)], wup_v[up_rows(t), span], preferred_element_type=F32)
        out_v[:, span] = y.astype(BF16)
        c = pltpu.make_async_copy(out_v.at[:, span], out.at[:, span], st_sem.at[p])
        c.start()
        stores.append(c)
    for c in stores:
        c.wait()
    for c in sends:
        c.wait_send()


def local(tokens, gate_values, routes, w_down, expert_gate, expert_up, expert_down, w_up):
    rows, top = routes.shape
    lat = w_down.shape[1]
    n_exp = lax.axis_size("expert")
    n_ten = lax.axis_size("tensor")
    exp_dev = expert_gate.shape[0]
    total = n_exp * exp_dev
    cap = n_ten * ((3 * rows * top + 2 * total * n_ten - 1) // (2 * total * n_ten))
    lw = lat // n_ten
    width = w_up.shape[1]
    dma = pltpu.SemaphoreType.DMA
    any_spec = pl.BlockSpec(memory_space=pl.ANY)
    vmem = pl.BlockSpec(memory_space=pltpu.VMEM)
    return pl.pallas_call(
        functools.partial(kernel, n_exp, n_ten, cap),
        out_shape=jax.ShapeDtypeStruct((rows, width), BF16),
        in_specs=[any_spec, vmem, vmem] + [any_spec] * 5,
        out_specs=any_spec,
        scratch_shapes=[
            pltpu.VMEM(tokens.shape, BF16),
            pltpu.VMEM(w_down.shape, BF16),
            pltpu.VMEM(expert_gate.shape[1:], BF16),
            pltpu.VMEM(expert_up.shape[1:], BF16),
            pltpu.VMEM(expert_down.shape[1:], BF16),
            pltpu.VMEM(w_up.shape, BF16),
            pltpu.VMEM((n_ten, rows, lw), BF16),
            pltpu.VMEM((n_ten, rows, lw), BF16),
            pltpu.VMEM((n_exp, cap, lw), BF16),
            pltpu.VMEM((n_exp, cap, lat), BF16),
            pltpu.VMEM((n_exp, cap, lw), F32),
            pltpu.VMEM((n_exp, n_ten, cap, lw), BF16),
            pltpu.VMEM((n_exp, n_ten, cap, lw), BF16),
            pltpu.VMEM((n_exp, cap, lw), BF16),
            pltpu.VMEM((n_exp, cap, lw), BF16),
            pltpu.VMEM((rows, lat), BF16),
            pltpu.VMEM((rows, width), F32),
            pltpu.VMEM((rows, width), BF16),
            dma((6 + n_ten,)),
            dma((n_ten,)), dma((n_ten,)),
            dma((n_exp,)), dma((n_exp,)),
            dma((n_exp, n_ten)), dma((n_exp, n_ten)),
            dma((n_exp, n_ten)), dma((n_exp, n_ten)),
            dma((n_exp,)), dma((n_exp,)),
            dma((n_ten,)), dma((n_ten,)),
            dma((2,)),
        ],
        compiler_params=pltpu.CompilerParams(
            collective_id=0, has_side_effects=True, vmem_limit_bytes=56 * 1024 * 1024
        ),
        name="moe_layer",
    )(tokens, gate_values.T, routes.T, w_down, expert_gate, expert_up, expert_down, w_up)


def solution(mesh):
    return jax.shard_map(
        local,
        mesh=mesh,
        in_specs=(
            P(("groups", "expert", "seq"), "tensor"),
            P(("groups", "expert", "seq"), None),
            P(("groups", "expert", "seq"), None),
            P("tensor", None),
            P("expert", None, "tensor"),
            P("expert", None, "tensor"),
            P("expert", "tensor", None),
            P(None, "tensor"),
        ),
        out_specs=P(("groups", "expert", "seq"), "tensor"),
        check_vma=False,
    )
```
